32 devices in a mesh: diff: 16 (over z, x, core), obj: 2 (over y).
Axes of the slice: x: 2, y: 2, z: 4, core: 2. Of those that a mesh axis runs over, the one named last changes fastest.
Arguments:
- object_field: float32 [2, 4096, 512], P(None, ('diff', 'obj')), may hold values from -6 to 6
- probe_modes: float32 [4, 2, 256, 256], P('obj'), may hold values from -3 to 3
- amplitudes: float32 [32, 256, 256], P('diff')
- offsets: int32 [32, 2], P('diff'), may hold values from 0 to 256, as said below
- counts: int32 [16], replicated, may hold values from 1 to 2, as said below
Outputs:
- object_out: float32 [2, 4096, 512], P(None, ('diff', 'obj'))
- probe_out: float32 [4, 2, 256, 256], P('obj')
The draws below stay inside these ranges and needn't reach their ends.
Inputs may be any that keep to these rules, and one draw needn't show every extreme that they name: Row k of offsets holds the block-local corner of slot k (block k // 2): offsets[k,0] < 256, and offsets[k,0] <= 0 in the last block; offsets[k,1] <= 256. Every slot, used or not, holds such a corner. Block b uses its first counts[b] slots.
All inputs are finite; a program needn't handle non-finite values.
Results may differ from the reference program's by a relative error of at most 0.0003.
Values sent between devices are 32-bit elements; how exact they have to be, the bound alone decides.
A program may use at most 64 MiB of HBM per device.

```python
import jax
import jax.numpy as jnp
from jax import lax

PATCH = 256
MODES = 4
SLOTS = 2
TILE_ROWS = 128
COLUMNS = 512
ITERS = 1
PASSES = 3
BLOCK_ROWS = 256
OBJ_ROWS = 4096
POSITIONS = 32
N_DIFF = 16
N_OBJ = 2


def draw_offsets(key, part):
    block_rows = TILE_ROWS * N_OBJ
    positions = jnp.arange(POSITIONS, dtype=jnp.int32)
    block_index = positions // SLOTS
    upper_rows = jnp.where(block_index == N_DIFF - 1, block_rows - PATCH + 1, block_rows)
    rows_drawn = jax.random.randint(jax.random.fold_in(key, 11), (POSITIONS,), 0, upper_rows)
    cols_drawn = jax.random.randint(jax.random.fold_in(key, 12), (POSITIONS,), 0, COLUMNS - PATCH + 1)
    rows_drawn = rows_drawn.at[0].set(block_rows - 1)
    cols_drawn = cols_drawn.at[0].set(COLUMNS - PATCH)
    return jnp.stack([rows_drawn, cols_drawn], axis=1).astype(jnp.int32)


def draw_counts(key, part):
    values = jax.random.randint(jax.random.fold_in(key, 21), (N_DIFF,), 1, SLOTS + 1)
    values = values.at[0].set(SLOTS).at[1].set(1)
    return values.astype(jnp.int32)


def draw_amplitudes(key, part):
    block_index = jnp.arange(POSITIONS, dtype=jnp.int32) // SLOTS
    rising = 1.0 + 2.0 * block_index.astype(jnp.float32) / (N_DIFF - 1)
    shape_all = (POSITIONS, PATCH, PATCH)
    subkey = jax.random.fold_in(key, 31)
    base = jax.random.uniform(subkey, shape_all, minval=0.2, maxval=2.0)
    return (base * rising[:, None, None]).astype(jnp.float32)


def shard_levels(stream_key, shape, split, smallest, top_value):
    def one(axis_at, blocks):
        heights = jax.random.uniform(jax.random.fold_in(jax.random.fold_in(stream_key, 6), axis_at), (blocks,), jnp.float32, smallest / len(split), top_value / len(split))
        return jnp.repeat(jnp.exp(heights), shape[axis_at] // blocks).reshape((-1,) + (1,) * (len(shape) - axis_at - 1))

    loudness = one(*split[0])
    for cut in split[1:]:
        loudness = loudness * one(*cut)
    return loudness


def scatter_about(key, dims, width, most, split=(), kind=jnp.bfloat16):
    drawn = jax.random.normal(key, dims, jnp.float32) * width
    if len(split) > 0:
        drawn = shard_levels(key, dims, split, -0.22, 0.18) * drawn
    return jnp.clip(drawn, min=-most, max=most).astype(kind)


def setup_inputs(seed: int = 0) -> dict:
    keys = jax.random.split(jax.random.key(seed), 6)
    object_field = scatter_about(keys[0], (2, OBJ_ROWS, COLUMNS), 1.0, 6.0, ((1, 32),), jnp.float32)
    probe_modes = scatter_about(keys[1], (MODES, 2, PATCH, PATCH), 0.5, 3.0, ((0, 2),), jnp.float32)
    amplitudes = draw_amplitudes(jax.random.fold_in(keys[5], 71), 0)
    offsets = draw_offsets(jax.random.fold_in(keys[5], 71), 0)
    counts = draw_counts(jax.random.fold_in(keys[5], 71), 0)
    return dict(object_field=object_field, probe_modes=probe_modes, amplitudes=amplitudes, offsets=offsets, counts=counts)


EDGE_SCALE = 1.0
DIFFUSION_RATE = 0.2
OBJECT_STEP = 0.25
HIGHEST = lax.Precision.HIGHEST

def dft_tables(length):
    ladder = jnp.arange(length, dtype=jnp.int32)
    product = ladder[:, None] * ladder[None, :] % length
    angle = product.astype(jnp.float32) * (2.0 * jnp.pi / length)
    scaling = 1.0 / jnp.sqrt(jnp.float32(length))
    return (jnp.cos(angle) * scaling, jnp.sin(angle) * scaling)

def apply_left(table, stacked):
    return jnp.einsum('jk,mkl->mjl', table, stacked, precision=HIGHEST)

def apply_right(stacked, table):
    return jnp.einsum('mjk,kl->mjl', stacked, table, precision=HIGHEST)

def to_detector(real_part, imag_part, cosine, sine_table):
    mid_real = apply_left(cosine, real_part) + apply_left(sine_table, imag_part)
    mid_imag = apply_left(cosine, imag_part) - apply_left(sine_table, real_part)
    out_real = apply_right(mid_real, cosine) + apply_right(mid_imag, sine_table)
    out_imag = apply_right(mid_imag, cosine) - apply_right(mid_real, sine_table)
    return (out_real, out_imag)

def to_sample(real_part, imag_part, cosine, sine_table):
    mid_real = apply_left(cosine, real_part) - apply_left(sine_table, imag_part)
    mid_imag = apply_left(cosine, imag_part) + apply_left(sine_table, real_part)
    out_real = apply_right(mid_real, cosine) - apply_right(mid_imag, sine_table)
    out_imag = apply_right(mid_imag, cosine) + apply_right(mid_real, sine_table)
    return (out_real, out_imag)

def detector_waves(patch_field, probe_modes, cosine, sine_table):
    probe_real = probe_modes[:, 0]
    probe_imag = probe_modes[:, 1]
    wave_real = probe_real * patch_field[0] - probe_imag * patch_field[1]
    wave_imag = probe_real * patch_field[1] + probe_imag * patch_field[0]
    far_real, far_imag = to_detector(wave_real, wave_imag, cosine, sine_table)
    return (far_real, far_imag, lax.optimization_barrier(jnp.sum(far_real * far_real + far_imag * far_imag, axis=0)))

def gradients(patch_field, probe_modes, far_real, far_imag, power, amplitude, cosine, sine_table):
    factor = amplitude / jnp.sqrt(power + 1.0) - 1.0
    back_real, back_imag = to_sample(far_real * factor, far_imag * factor, cosine, sine_table)
    probe_real = probe_modes[:, 0]
    probe_imag = probe_modes[:, 1]
    patch_grad = jnp.stack([lax.optimization_barrier(jnp.sum(probe_real * back_real + probe_imag * back_imag, axis=0)), lax.optimization_barrier(jnp.sum(probe_real * back_imag - probe_imag * back_real, axis=0))])
    probe_grad = jnp.stack([patch_field[0] * back_real + patch_field[1] * back_imag, patch_field[0] * back_imag - patch_field[1] * back_real], axis=1)
    return (patch_grad, probe_grad)

def edge_flux(difference):
    weight = 1.0 / (1.0 + lax.optimization_barrier(jnp.sum(difference * difference, axis=0, keepdims=True)) / (EDGE_SCALE * EDGE_SCALE))
    return difference * weight

def diffuse(stacked, row_ids, total_rows):
    center = stacked[:, 1:-1]
    inner_ids = row_ids[1:-1]
    valid_up = ((inner_ids >= 1) & (inner_ids <= total_rows)).astype(stacked.dtype)
    valid_down = ((inner_ids >= -1) & (inner_ids < total_rows - 1)).astype(stacked.dtype)
    upward = edge_flux(stacked[:, :-2] - center) * valid_up[None, :, None]
    downward = edge_flux(stacked[:, 2:] - center) * valid_down[None, :, None]
    across = edge_flux(center[:, :, 1:] - center[:, :, :-1])
    zero_column = jnp.zeros_like(center[:, :, :1])
    sideways = jnp.concatenate([across, zero_column], axis=2) - jnp.concatenate([zero_column, across], axis=2)
    return center + DIFFUSION_RATE * (upward + downward + sideways)

def reference(object_field, probe_modes, amplitudes, offsets, counts):
    cosine, sine_table = dft_tables(PATCH)
    total_rows = BLOCK_ROWS * N_DIFF
    for iteration in range(ITERS):
        padded = jnp.concatenate([object_field, jnp.zeros((2, PATCH, COLUMNS), object_field.dtype)], axis=1)

        def visit(carry, slot):
            grand, probe_sum = carry
            block_index = slot // SLOTS
            row = block_index * BLOCK_ROWS + offsets[slot, 0]
            column = offsets[slot, 1]
            anchor = (jnp.int32(0), row, column)
            patch_field = lax.dynamic_slice(padded, anchor, (2, PATCH, PATCH))
            far_real, far_imag, power = detector_waves(patch_field, probe_modes, cosine, sine_table)
            patch_grad, probe_grad = gradients(patch_field, probe_modes, far_real, far_imag, power, amplitudes[slot], cosine, sine_table)
            weight = (slot % SLOTS < counts[block_index]).astype(object_field.dtype)
            current = lax.dynamic_slice(grand, anchor, (2, PATCH, PATCH))
            grand = lax.dynamic_update_slice(grand, current + weight * patch_grad, anchor)
            return ((grand, probe_sum + weight * probe_grad), None)
        start = (jnp.zeros_like(padded), jnp.zeros_like(probe_modes))
        (grand, probe_sum), unused = lax.scan(visit, start, jnp.arange(N_DIFF * SLOTS, dtype=jnp.int32))
        smooth = object_field + OBJECT_STEP * grand[:, :total_rows]
        row_ids = jnp.arange(-1, total_rows + 1, dtype=jnp.int32)
        for sweep in range(PASSES):
            smooth = diffuse(jnp.pad(smooth, ((0, 0), (1, 1), (0, 0))), row_ids, total_rows)
        object_field = smooth
        probe_modes = probe_modes + probe_sum / N_DIFF
    return (object_field, probe_modes)
```

```python
import functools

import jax
import jax.numpy as jnp
import ml_dtypes
import numpy as np
from jax import lax
from jax.experimental import pallas as pl
from jax.experimental.pallas import tpu as pltpu
from jax.sharding import PartitionSpec as P

PASSES = 3
EDGE_SCALE = 1.0
DIFFUSION_RATE = 0.2
OBJECT_STEP = 0.25
EDGE = 8
MESH = pl.DeviceIdType.MESH
BF16 = jnp.bfloat16
F32 = jnp.float32


def dft_blocks(length):
    ladder = np.arange(length)
    angle = (ladder[:, None] * ladder[None, :] % length) * (2.0 * np.pi / length)
    cosine = np.cos(angle) / np.sqrt(length)
    sine = np.sin(angle) / np.sqrt(length)
    forward = np.block([[cosine, sine], [-sine, cosine]]).astype(np.float32)

    def halves(table):
        high = table.astype(ml_dtypes.bfloat16)
        low = (table - high.astype(np.float32)).astype(ml_dtypes.bfloat16)
        return np.stack([high, low])

    return np.stack([halves(forward), halves(forward.T)])


def split(value):
    high = value.astype(BF16)
    return high, (value - high.astype(F32)).astype(BF16)


def dot(a, b):
    return jnp.dot(a, b, preferred_element_type=F32)


def transform(real, imag, tables, left, right, length):
    high, low = split(jnp.concatenate([real, imag], axis=0))
    mid = dot(tables[left, 0], high) + dot(tables[left, 0], low) + dot(tables[left, 1], high)
    high, low = split(jnp.concatenate([mid[:length], mid[length:]], axis=1))
    out = dot(high, tables[right, 0]) + dot(low, tables[right, 0]) + dot(high, tables[right, 1])
    return out


def flux_of(real, imag):
    weight = 1.0 / (1.0 + (real * real + imag * imag) / (EDGE_SCALE * EDGE_SCALE))
    return real * weight, imag * weight


def kernel(n, obj_ref, probe_ref, amp_ref, off_ref, cnt_ref, tab_ref, out_ref, pout_ref,
           ext, pf, far, pw, pw_in, gext, patch, spill, ysend, yin, mar, ps, rbuf, po, ssem, rsem):
    tile, columns = obj_ref.shape[1:]
    length = pf.shape[-1]
    slots, modes = pf.shape[0], probe_ref.shape[0]
    block = 2 * tile
    bits = n.bit_length() - 1
    d, o = lax.axis_index("diff"), lax.axis_index("obj")
    q = 1 - o
    has_low, has_high = d > 0, d < n - 1
    rank = 2 * d + o
    has_prev, has_next = rank > 0, rank < 2 * n - 1
    partner = {"diff": d, "obj": q}
    lower = {"diff": d - 1, "obj": o}
    upper = {"diff": d + 1, "obj": o}
    prev_tile = {"diff": d - 1 + o, "obj": q}
    next_tile = {"diff": d + o, "obj": q}
    bit = [lax.rem(d // (1 << k), 2) for k in range(bits)]
    cube = [{"diff": d + (1 - 2 * bit[k]) * (1 << k), "obj": o} for k in range(bits)]

    def remote(src, dst, index, device):
        return pltpu.make_async_remote_copy(
            src_ref=src, dst_ref=dst, send_sem=ssem.at[index], recv_sem=rsem.at[index],
            device_id=device, device_id_type=MESH)

    def rows(start, size):
        return pl.ds(pl.multiple_of(start, 8), size)

    def pick(shape, long, offset):
        far_at = lax.broadcasted_iota(jnp.int32, shape, long)
        near_at = lax.broadcasted_iota(jnp.int32, shape, 1 - long)
        return jnp.where(far_at - near_at == offset, 1.0, 0.0).astype(BF16)

    barrier = pltpu.get_barrier_semaphore()

    def greet(device):
        pl.semaphore_signal(barrier, inc=1, device_id=device, device_id_type=MESH)

    greet(partner)
    for k in range(bits):
        greet(cube[k])
    other = d - 1 + 2 * bit[0]
    cross = d - 1 + 2 * o
    has_other = (other >= 0) & (other < n)
    has_cross = (cross >= 0) & (cross < n)

    @pl.when(has_other)
    def _():
        greet({"diff": other, "obj": o})

    @pl.when(has_cross)
    def _():
        greet({"diff": cross, "obj": q})

    pl.semaphore_wait(barrier, 1 + bits + has_other.astype(jnp.int32) + has_cross.astype(jnp.int32))

    to_partner, direct, relay = [], [], []
    for c in range(2):
        to_partner.append(remote(obj_ref.at[c], ext.at[c, rows(o * tile, tile)], c, partner))
        direct.append(remote(obj_ref.at[c], ext.at[c, rows(block + o * tile, tile)], 2 + c, lower))
        relay.append(remote(ext.at[c, rows(q * tile, tile)], ext.at[c, rows(block + q * tile, tile)], 4 + c, lower))
        to_partner[c].start()
    for c in range(2):
        pl.when(has_low)(direct[c].start)
    for c in range(2):
        ext[c, rows(o * tile, tile), :] = obj_ref[c]

    @pl.when(d == n - 1)
    def _():
        for c in range(2):
            ext[c, block:, :] = jnp.zeros((block, columns), F32)

    @pl.when(d == 0)
    def _():
        spill[...] = jnp.zeros_like(spill)

    @pl.when(rank == 0)
    def _():
        mar[:, :EDGE, :] = jnp.zeros((2, EDGE, columns), F32)

    @pl.when(rank == 2 * n - 1)
    def _():
        mar[:, EDGE + tile:, :] = jnp.zeros((2, EDGE, columns), F32)

    for c in range(2):
        to_partner[c].wait_recv()
        pl.when(has_low)(relay[c].start)
    for c in range(2):
        pl.when(has_high)(direct[c].wait_recv)
    for c in range(2):
        pl.when(has_high)(relay[c].wait_recv)

    power_copy = []
    for s in range(slots):
        row_pick = pick((length, 2 * block), 1, off_ref[s, 0])
        column_pick = pick((columns, length), 0, off_ref[s, 1])
        for c in range(2):
            high, low = split(ext[c])
            high, low = split(dot(high, column_pick) + dot(low, column_pick))
            pf[s, c] = dot(row_pick, high) + dot(row_pick, low)
        pw[s] = jnp.zeros((length, length), F32)

        @pl.loop(0, modes)
        def _(m, s=s):
            pr, pi = probe_ref[m, 0], probe_ref[m, 1]
            fr, fi = pf[s, 0], pf[s, 1]
            wave = transform(pr * fr - pi * fi, pr * fi + pi * fr, tab_ref, 0, 1, length)
            far[s, m] = wave
            real, imag = wave[:, :length], wave[:, length:]
            pw[s] += real * real + imag * imag

        power_copy.append(remote(pw.at[s], pw_in.at[s], 6 + s, partner))
        power_copy[s].start()

    base = 6 + slots
    for s in range(slots):
        used = jnp.full((1, length), cnt_ref[d], jnp.int32)
        weight = jnp.where(used > s, 1.0, 0.0).astype(F32)
        power_copy[s].wait_recv()
        patch[...] = jnp.zeros_like(patch)
        pw_in[s] = amp_ref[s] / jnp.sqrt(pw[s] + pw_in[s] + 1.0) - 1.0

        @pl.loop(0, modes)
        def _(m, s=s, weight=weight):
            pr, pi = probe_ref[m, 0], probe_ref[m, 1]
            fr, fi = pf[s, 0], pf[s, 1]
            factor = pw_in[s]
            back = transform(far[s, m, :, :length] * factor, far[s, m, :, length:] * factor,
                             tab_ref, 1, 0, length)
            real, imag = back[:, :length] * weight, back[:, length:] * weight
            patch[0] += pr * real + pi * imag
            patch[1] += pr * imag - pi * real
            grad_r = fr * real + fi * imag
            grad_i = fr * imag - fi * real
            at_r = rows(m * 2 * length, length)
            at_i = rows(m * 2 * length + length, length)
            if s == 0:
                ps[at_r, :] = grad_r
                ps[at_i, :] = grad_i
            else:
                ps[at_r, :] += grad_r
                ps[at_i, :] += grad_i

        row_place = pick((2 * block, length), 0, off_ref[s, 0])
        column_place = pick((length, columns), 1, off_ref[s, 1])
        for c in range(2):
            high, low = split(patch[c])
            high, low = split(dot(row_place, high) + dot(row_place, low))
            placed = dot(high, column_place) + dot(low, column_place)
            if s == 0:
                gext[c] = placed
            else:
                gext[c] += placed

    spill_copy = [remote(gext.at[:, rows(block + t * tile, tile)], spill.at[h], base + h, upper)
                  for h, t in ((0, q), (1, o))]
    for copy in spill_copy:
        pl.when(has_high)(copy.start)

    sums_at, share_at = base + 5, base + 5 + bits
    total = ps.shape[0]
    starts, sizes = [jnp.int32(0)], [total]
    sums, shares = [], []
    filled = 0
    for k in range(bits):
        half = sizes[k] // 2
        sums.append(remote(ps.at[rows(starts[k] + (1 - bit[k]) * half, half)], rbuf.at[pl.ds(filled, half)],
                           sums_at + k, cube[k]))
        starts.append(starts[k] + bit[k] * half)
        sizes.append(half)
        filled += half
    for k in range(bits):
        mine = po.at[rows(starts[k + 1], sizes[k + 1])]
        shares.append(remote(mine, mine, share_at + k, cube[k]))

    def add_sum(k):
        sums[k].wait_recv()
        at = total - sizes[k]
        keep = rows(starts[k + 1], sizes[k + 1])
        ps[keep, :] += rbuf[at:at + sizes[k + 1], :]

    sums[0].start()
    pl.when(has_low)(spill_copy[0].wait_recv)
    ysend[...] = gext[:, rows(q * tile, tile), :] + spill[0]
    to_owner = remote(ysend, yin, base + 2, partner)
    to_owner.start()
    for k in range(bits):
        add_sum(k)
        if k + 1 < bits:
            sums[k + 1].start()
    last = rows(starts[bits], sizes[bits])
    po[last, :] = ps[last, :]
    shares[bits - 1].start()

    pl.when(has_low)(spill_copy[1].wait_recv)
    to_owner.wait_recv()
    mar[:, EDGE:EDGE + tile, :] = obj_ref[...] + OBJECT_STEP * (gext[:, rows(o * tile, tile), :] + spill[1] + yin[...])
    up = remote(mar.at[:, pl.ds(EDGE, EDGE)], mar.at[:, pl.ds(EDGE + tile, EDGE)], base + 3, prev_tile)
    down = remote(mar.at[:, pl.ds(tile, EDGE)], mar.at[:, pl.ds(0, EDGE)], base + 4, next_tile)
    pl.when(has_prev)(up.start)
    pl.when(has_next)(down.start)
    left = list(range(bits - 1, -1, -1))

    def share():
        if left:
            k = left.pop(0)
            shares[k].wait_recv()
            if left:
                shares[left[0]].start()

    share()
    pl.when(has_next)(up.wait_recv)
    pl.when(has_prev)(down.wait_recv)

    tall = tile + 2 * EDGE
    ids = rank * tile - EDGE + lax.broadcasted_iota(jnp.int32, (tall, columns), 0)
    below = (ids >= 0) & (ids + 1 < 2 * n * tile)
    beside = lax.broadcasted_iota(jnp.int32, (tall, columns), 1) < columns - 1
    u_r, u_i = mar[0], mar[1]
    for sweep in range(PASSES):
        v_r, v_i = flux_of(pltpu.roll(u_r, tall - 1, 0) - u_r, pltpu.roll(u_i, tall - 1, 0) - u_i)
        h_r, h_i = flux_of(pltpu.roll(u_r, columns - 1, 1) - u_r, pltpu.roll(u_i, columns - 1, 1) - u_i)

        def moved(v, h):
            v = jnp.where(below, v, 0.0)
            h = jnp.where(beside, h, 0.0)
            return DIFFUSION_RATE * ((v - pltpu.roll(v, 1, 0)) + (h - pltpu.roll(h, 1, 1)))

        u_r, u_i = u_r + moved(v_r, h_r), u_i + moved(v_i, h_i)
        share()
    out_ref[0] = u_r[EDGE:EDGE + tile]
    out_ref[1] = u_i[EDGE:EDGE + tile]
    while left:
        share()
    for m in range(modes):
        for c in range(2):
            at = (m * 2 + c) * length
            pout_ref[m, c] = probe_ref[m, c] + po[at:at + length, :] / n

    for copy in to_partner + power_copy + sums + shares + [to_owner]:
        copy.wait_send()
    for copy in direct + relay:
        pl.when(has_low)(copy.wait_send)
    for copy in spill_copy:
        pl.when(has_high)(copy.wait_send)
    pl.when(has_prev)(up.wait_send)
    pl.when(has_next)(down.wait_send)


def body(n, object_field, probe_modes, amplitudes, offsets, counts):
    _, tile, columns = object_field.shape
    modes, _, length, _ = probe_modes.shape
    slots = amplitudes.shape[0]
    bits = n.bit_length() - 1
    block = 2 * tile
    copies = 11 + slots + 2 * bits
    vmem = pl.BlockSpec(memory_space=pltpu.VMEM)
    smem = pl.BlockSpec(memory_space=pltpu.SMEM)
    tables = jnp.asarray(dft_blocks(length))
    return pl.pallas_call(
        functools.partial(kernel, n),
        out_shape=(
            jax.ShapeDtypeStruct(object_field.shape, F32),
            jax.ShapeDtypeStruct(probe_modes.shape, F32),
        ),
        in_specs=[vmem, vmem, vmem, smem, smem, vmem],
        out_specs=(vmem, vmem),
        scratch_shapes=[
            pltpu.VMEM((2, 2 * block, columns), F32),
            pltpu.VMEM((slots, 2, length, length), F32),
            pltpu.VMEM((slots, modes, length, 2 * length), F32),
            pltpu.VMEM((slots, length, length), F32),
            pltpu.VMEM((slots, length, length), F32),
            pltpu.VMEM((2, 2 * block, columns), F32),
            pltpu.VMEM((2, length, length), F32),
            pltpu.VMEM((2, 2, tile, columns), F32),
            pltpu.VMEM((2, tile, columns), F32),
            pltpu.VMEM((2, tile, columns), F32),
            pltpu.VMEM((2, tile + 2 * EDGE, columns), F32),
            pltpu.VMEM((modes * 2 * length, length), F32),
            pltpu.VMEM((modes * 2 * length, length), F32),
            pltpu.VMEM((modes * 2 * length, length), F32),
            pltpu.SemaphoreType.DMA((copies,)),
            pltpu.SemaphoreType.DMA((copies,)),
        ],
        compiler_params=pltpu.CompilerParams(
            collective_id=0, has_side_effects=True, vmem_limit_bytes=48 * 2**20
        ),
    )(object_field, probe_modes, amplitudes, offsets, counts, tables)


def solution(mesh):
    placed = (
        P(None, ("diff", "obj"), None),
        P("obj", None, None, None),
        P("diff", None, None),
        P("diff", None),
        P(),
    )
    return jax.shard_map(
        functools.partial(body, mesh.shape["diff"]),
        mesh=mesh,
        in_specs=placed,
        out_specs=(P(None, ("diff", "obj"), None), P("obj", None, None, None)),
        check_vma=False,
    )
```

```python
import functools

import jax
import jax.numpy as jnp
import ml_dtypes
import numpy as np
from jax import lax
from jax.experimental import pallas as pl
from jax.experimental.pallas import tpu as pltpu
from jax.sharding import PartitionSpec as P

PASSES = 3
EDGE_SCALE = 1.0
DIFFUSION_RATE = 0.2
OBJECT_STEP = 0.25
EDGE = 8
LANES = 128
MESH = pl.DeviceIdType.MESH
BF16 = jnp.bfloat16
F32 = jnp.float32


def dft_blocks(length):
    ladder = np.arange(length)
    angle = (ladder[:, None] * ladder[None, :] % length) * (2.0 * np.pi / length)
    cosine = np.cos(angle) / np.sqrt(length)
    sine = np.sin(angle) / np.sqrt(length)
    forward = np.block([[cosine, sine], [-sine, cosine]]).astype(np.float32)

    def halves(table):
        high = table.astype(ml_dtypes.bfloat16)
        low = (table - high.astype(np.float32)).astype(ml_dtypes.bfloat16)
        return np.stack([high, low])

    return np.stack([halves(forward), halves(forward.T)])


def split(value):
    high = value.astype(BF16)
    return high, (value - high.astype(F32)).astype(BF16)


def dot(a, b):
    return jnp.dot(a, b, preferred_element_type=F32)


def transform(real, imag, tables, left, right, length):
    high, low = split(jnp.concatenate([real, imag], axis=0))
    mid = dot(tables[left, 0], high) + dot(tables[left, 0], low) + dot(tables[left, 1], high)
    high, low = split(jnp.concatenate([mid[:length], mid[length:]], axis=1))
    out = dot(high, tables[right, 0]) + dot(low, tables[right, 0]) + dot(high, tables[right, 1])
    return out


def flux_of(real, imag):
    weight = 1.0 / (1.0 + (real * real + imag * imag) / (EDGE_SCALE * EDGE_SCALE))
    return real * weight, imag * weight


def kernel(n, obj_in, probe_in, amp_in, off_ref, cnt_ref, tab_in, out_ref, pout_ref,
           obj_ref, probe_ref, amp_ref, tab_ref, load_sem, ext, pf, far, pw, pw_in, gext, patch, spill, ysend, yin, mar, ps, rbuf, po, ssem, rsem):
    tile, columns = obj_ref.shape[1:]
    length = pf.shape[-1]
    slots, modes = pf.shape[0], probe_ref.shape[0]
    block = 2 * tile
    bits = n.bit_length() - 1
    strips = length // LANES
    d, o = lax.axis_index("diff"), lax.axis_index("obj")
    q = 1 - o
    has_low, has_high = d > 0, d < n - 1
    rank = 2 * d + o
    has_prev, has_next = rank > 0, rank < 2 * n - 1
    partner = {"diff": d, "obj": q}
    lower = {"diff": d - 1, "obj": o}
    upper = {"diff": d + 1, "obj": o}
    prev_tile = {"diff": d - 1 + o, "obj": q}
    next_tile = {"diff": d + o, "obj": q}
    bit = [lax.rem(d // (1 << k), 2) for k in range(bits)]
    cube = [{"diff": d + (1 - 2 * bit[k]) * (1 << k), "obj": o} for k in range(bits)]

    def remote(src, dst, index, device):
        return pltpu.make_async_remote_copy(
            src_ref=src, dst_ref=dst, send_sem=ssem.at[index], recv_sem=rsem.at[index],
            device_id=device, device_id_type=MESH)

    def rows(start, size):
        return pl.ds(pl.multiple_of(start, 8), size)

    def pick(shape, long, offset):
        far_at = lax.broadcasted_iota(jnp.int32, shape, long)
        near_at = lax.broadcasted_iota(jnp.int32, shape, 1 - long)
        return jnp.where(far_at - near_at == offset, 1.0, 0.0).astype(BF16)

    loads = [pltpu.make_async_copy(src, dst, load_sem.at[i]) for i, (src, dst) in enumerate(
        ((obj_in, obj_ref), (tab_in, tab_ref), (probe_in, probe_ref), (amp_in, amp_ref)))]
    for load in loads:
        load.start()

    barrier = pltpu.get_barrier_semaphore()

    def greet(device):
        pl.semaphore_signal(barrier, inc=1, device_id=device, device_id_type=MESH)

    greet(partner)
    for k in range(bits):
        greet(cube[k])
    other = d - 1 + 2 * bit[0]
    cross = d - 1 + 2 * o
    has_other = (other >= 0) & (other < n)
    has_cross = (cross >= 0) & (cross < n)

    @pl.when(has_other)
    def _():
        greet({"diff": other, "obj": o})

    @pl.when(has_cross)
    def _():
        greet({"diff": cross, "obj": q})

    pl.semaphore_wait(barrier, 1 + bits + has_other.astype(jnp.int32) + has_cross.astype(jnp.int32))

    to_partner, direct, relay = [], [], []
    for c in range(2):
        to_partner.append(remote(obj_in.at[c], ext.at[c, rows(o * tile, tile)], c, partner))
        direct.append(remote(obj_in.at[c], ext.at[c, rows(block + o * tile, tile)], 2 + c, lower))
        relay.append(remote(ext.at[c, rows(q * tile, tile)], ext.at[c, rows(block + q * tile, tile)], 4 + c, lower))
        to_partner[c].start()
    for c in range(2):
        pl.when(has_low)(direct[c].start)
    for load in loads:
        load.wait()
    for c in range(2):
        ext[c, rows(o * tile, tile), :] = obj_ref[c]

    @pl.when(d == n - 1)
    def _():
        for c in range(2):
            ext[c, block:, :] = jnp.zeros((block, columns), F32)

    @pl.when(d == 0)
    def _():
        spill[...] = jnp.zeros_like(spill)

    @pl.when(rank == 0)
    def _():
        mar[:, :EDGE, :] = jnp.zeros((2, EDGE, columns), F32)

    @pl.when(rank == 2 * n - 1)
    def _():
        mar[:, EDGE + tile:, :] = jnp.zeros((2, EDGE, columns), F32)

    for c in range(2):
        to_partner[c].wait_recv()
        pl.when(has_low)(relay[c].start)
    for c in range(2):
        pl.when(has_high)(direct[c].wait_recv)
    for c in range(2):
        pl.when(has_high)(relay[c].wait_recv)

    base = 6 + slots
    total = ps.shape[0] // modes
    sums, shares, keeps, places = [], [], [], []
    index = base + 5
    for g in range(modes):
        rest = list(range(1, bits))
        turn = g % max(1, len(rest))
        order = [0] + rest[turn:] + rest[:turn]
        start, size, filled = g * total, total, g * total
        sums.append([])
        shares.append([])
        keeps.append([])
        places.append([])
        for k in order:
            half = size // 2
            sums[g].append(remote(ps.at[rows(start + (1 - bit[k]) * half, half)],
                                  rbuf.at[pl.ds(filled, half)], index, cube[k]))
            places[g].append((filled, half))
            start, size = start + bit[k] * half, half
            keeps[g].append(rows(start, size))
            filled += half
            index += 1
        for step, k in enumerate(order):
            mine = po.at[keeps[g][step]]
            shares[g].append(remote(mine, mine, index, cube[k]))
            index += 1

    power_copy = []
    for s in range(slots):
        row_pick = pick((length, 2 * block), 1, off_ref[s, 0])
        column_pick = pick((columns, length), 0, off_ref[s, 1])
        for c in range(2):
            high, low = split(ext[c])
            high, low = split(dot(high, column_pick) + dot(low, column_pick))
            pf[s, c] = dot(row_pick, high) + dot(row_pick, low)
        pw[s] = jnp.zeros((length, length), F32)

        @pl.loop(0, modes)
        def _(m, s=s):
            pr, pi = probe_ref[m, 0], probe_ref[m, 1]
            fr, fi = pf[s, 0], pf[s, 1]
            wave = transform(pr * fr - pi * fi, pr * fi + pi * fr, tab_ref, 0, 1, length)
            far[s, m] = wave
            real, imag = wave[:, :length], wave[:, length:]
            pw[s] += real * real + imag * imag

        power_copy.append(remote(pw.at[s], pw_in.at[s], 6 + s, partner))
        power_copy[s].start()

    for s in range(slots):
        used = jnp.full((1, length), cnt_ref[d], jnp.int32)
        weight = jnp.where(used > s, 1.0, 0.0).astype(F32)
        power_copy[s].wait_recv()
        patch[...] = jnp.zeros_like(patch)
        pw_in[s] = amp_ref[s] / jnp.sqrt(pw[s] + pw_in[s] + 1.0) - 1.0

        @pl.loop(0, modes)
        def _(m, s=s, weight=weight):
            pr, pi = probe_ref[m, 0], probe_ref[m, 1]
            fr, fi = pf[s, 0], pf[s, 1]
            factor = pw_in[s]
            back = transform(far[s, m, :, :length] * factor, far[s, m, :, length:] * factor,
                             tab_ref, 1, 0, length)
            real, imag = back[:, :length] * weight, back[:, length:] * weight
            patch[0] += pr * real + pi * imag
            patch[1] += pr * imag - pi * real
            grad_r = fr * real + fi * imag
            grad_i = fr * imag - fi * real
            for c, grad in ((0, grad_r), (1, grad_i)):
                for h in range(strips):
                    at = rows(((m * 2 + c) * strips + h) * length, length)
                    if s == 0:
                        ps[at, :] = grad[:, h * LANES:(h + 1) * LANES]
                    else:
                        ps[at, :] += grad[:, h * LANES:(h + 1) * LANES]

        if s == slots - 1:
            for g in range(modes):
                sums[g][0].start()
        row_place = pick((2 * block, length), 0, off_ref[s, 0])
        column_place = pick((length, columns), 1, off_ref[s, 1])
        for c in range(2):
            high, low = split(patch[c])
            high, low = split(dot(row_place, high) + dot(row_place, low))
            placed = dot(high, column_place) + dot(low, column_place)
            if s == 0:
                gext[c] = placed
            else:
                gext[c] += placed

    spill_copy = [remote(gext.at[:, rows(block + t * tile, tile)], spill.at[h], base + h, upper)
                  for h, t in ((0, q), (1, o))]
    for copy in spill_copy:
        pl.when(has_high)(copy.start)

    def add_sum(g, k):
        sums[g][k].wait_recv()
        at, size = places[g][k]
        ps[keeps[g][k], :] += rbuf[at:at + size, :]

    pl.when(has_low)(spill_copy[0].wait_recv)
    ysend[...] = gext[:, rows(q * tile, tile), :] + spill[0]
    to_owner = remote(ysend, yin, base + 2, partner)
    to_owner.start()
    for k in range(bits):
        for g in range(modes):
            add_sum(g, k)
            if k + 1 < bits:
                sums[g][k + 1].start()
            else:
                po[keeps[g][k], :] = ps[keeps[g][k], :]
                shares[g][k].start()

    pl.when(has_low)(spill_copy[1].wait_recv)
    to_owner.wait_recv()
    mar[:, EDGE:EDGE + tile, :] = obj_ref[...] + OBJECT_STEP * (gext[:, rows(o * tile, tile), :] + spill[1] + yin[...])
    up = remote(mar.at[:, pl.ds(EDGE, EDGE)], mar.at[:, pl.ds(EDGE + tile, EDGE)], base + 3, prev_tile)
    down = remote(mar.at[:, pl.ds(tile, EDGE)], mar.at[:, pl.ds(0, EDGE)], base + 4, next_tile)
    pl.when(has_prev)(up.start)
    pl.when(has_next)(down.start)
    left = list(range(bits - 1, -1, -1))

    def share():
        if left:
            k = left.pop(0)
            for g in range(modes):
                shares[g][k].wait_recv()
                if left:
                    shares[g][left[0]].start()

    share()
    pl.when(has_next)(up.wait_recv)
    pl.when(has_prev)(down.wait_recv)

    tall = tile + 2 * EDGE
    ids = rank * tile - EDGE + lax.broadcasted_iota(jnp.int32, (tall, columns), 0)
    below = (ids >= 0) & (ids + 1 < 2 * n * tile)
    beside = lax.broadcasted_iota(jnp.int32, (tall, columns), 1) < columns - 1
    u_r, u_i = mar[0], mar[1]
    for sweep in range(PASSES):
        v_r, v_i = flux_of(pltpu.roll(u_r, tall - 1, 0) - u_r, pltpu.roll(u_i, tall - 1, 0) - u_i)
        h_r, h_i = flux_of(pltpu.roll(u_r, columns - 1, 1) - u_r, pltpu.roll(u_i, columns - 1, 1) - u_i)

        def moved(v, h):
            v = jnp.where(below, v, 0.0)
            h = jnp.where(beside, h, 0.0)
            return DIFFUSION_RATE * ((v - pltpu.roll(v, 1, 0)) + (h - pltpu.roll(h, 1, 1)))

        u_r, u_i = u_r + moved(v_r, h_r), u_i + moved(v_i, h_i)
        share()
    out_ref[0] = u_r[EDGE:EDGE + tile]
    out_ref[1] = u_i[EDGE:EDGE + tile]
    while left:
        share()
    for m in range(modes):
        for c in range(2):
            for h in range(strips):
                at = ((m * 2 + c) * strips + h) * length
                lanes = slice(h * LANES, (h + 1) * LANES)
                pout_ref[m, c, :, lanes] = probe_ref[m, c, :, lanes] + po[at:at + length, :] / n

    for copy in to_partner + power_copy + sum(sums, []) + sum(shares, []) + [to_owner]:
        copy.wait_send()
    for copy in direct + relay:
        pl.when(has_low)(copy.wait_send)
    for copy in spill_copy:
        pl.when(has_high)(copy.wait_send)
    pl.when(has_prev)(up.wait_send)
    pl.when(has_next)(down.wait_send)


def body(n, object_field, probe_modes, amplitudes, offsets, counts):
    _, tile, columns = object_field.shape
    modes, _, length, _ = probe_modes.shape
    slots = amplitudes.shape[0]
    bits = n.bit_length() - 1
    block = 2 * tile
    copies = 11 + slots + 2 * bits * modes
    vmem = pl.BlockSpec(memory_space=pltpu.VMEM)
    hbm = pl.BlockSpec(memory_space=pltpu.HBM)
    smem = pl.BlockSpec(memory_space=pltpu.SMEM)
    tables = jnp.asarray(dft_blocks(length))
    return pl.pallas_call(
        functools.partial(kernel, n),
        out_shape=(
            jax.ShapeDtypeStruct(object_field.shape, F32),
            jax.ShapeDtypeStruct(probe_modes.shape, F32),
        ),
        in_specs=[hbm, hbm, hbm, smem, smem, hbm],
        out_specs=(vmem, vmem),
        scratch_shapes=[
            pltpu.VMEM(object_field.shape, F32),
            pltpu.VMEM(probe_modes.shape, F32),
            pltpu.VMEM(amplitudes.shape, F32),
            pltpu.VMEM(tables.shape, BF16),
            pltpu.SemaphoreType.DMA((4,)),
            pltpu.VMEM((2, 2 * block, columns), F32),
            pltpu.VMEM((slots, 2, length, length), F32),
            pltpu.VMEM((slots, modes, length, 2 * length), F32),
            pltpu.VMEM((slots, length, length), F32),
            pltpu.VMEM((slots, length, length), F32),
            pltpu.VMEM((2, 2 * block, columns), F32),
            pltpu.VMEM((2, length, length), F32),
            pltpu.VMEM((2, 2, tile, columns), F32),
            pltpu.VMEM((2, tile, columns), F32),
            pltpu.VMEM((2, tile, columns), F32),
            pltpu.VMEM((2, tile + 2 * EDGE, columns), F32),
            pltpu.VMEM((modes * 2 * length * length // LANES, LANES), F32),
            pltpu.VMEM((modes * 2 * length * length // LANES, LANES), F32),
            pltpu.VMEM((modes * 2 * length * length // LANES, LANES), F32),
            pltpu.SemaphoreType.DMA((copies,)),
            pltpu.SemaphoreType.DMA((copies,)),
        ],
        compiler_params=pltpu.CompilerParams(
            collective_id=0, has_side_effects=True, vmem_limit_bytes=48 * 2**20
        ),
    )(object_field, probe_modes, amplitudes, offsets, counts, tables)


def solution(mesh):
    placed = (
        P(None, ("diff", "obj"), None),
        P("obj", None, None, None),
        P("diff", None, None),
        P("diff", None),
        P(),
    )
    return jax.shard_map(
        functools.partial(body, mesh.shape["diff"]),
        mesh=mesh,
        in_specs=placed,
        out_specs=(P(None, ("diff", "obj"), None), P("obj", None, None, None)),
        check_vma=False,
    )
```

```python
import functools

import jax
import jax.numpy as jnp
import ml_dtypes
import numpy as np
from jax import lax
from jax.experimental import pallas as pl
from jax.experimental.pallas import tpu as pltpu
from jax.sharding import PartitionSpec as P

PASSES = 3
EDGE_SCALE = 1.0
DIFFUSION_RATE = 0.2
OBJECT_STEP = 0.25
EDGE = 8
LANES = 128
MESH = pl.DeviceIdType.MESH
BF16 = jnp.bfloat16
F32 = jnp.float32


def dft_blocks(length):
    ladder = np.arange(length)
    angle = (ladder[:, None] * ladder[None, :] % length) * (2.0 * np.pi / length)
    cosine = np.cos(angle) / np.sqrt(length)
    sine = np.sin(angle) / np.sqrt(length)
    forward = np.block([[cosine, sine], [-sine, cosine]]).astype(np.float32)

    def halves(table):
        high = table.astype(ml_dtypes.bfloat16)
        low = (table - high.astype(np.float32)).astype(ml_dtypes.bfloat16)
        return np.stack([high, low])

    return np.stack([halves(forward), halves(forward.T)])


def split(value):
    high = value.astype(BF16)
    return high, (value - high.astype(F32)).astype(BF16)


def dot(a, b):
    return jnp.dot(a, b, preferred_element_type=F32)


def transform(real, imag, tables, left, right, length):
    high, low = split(jnp.concatenate([real, imag], axis=0))
    mid = dot(tables[left, 0], high) + dot(tables[left, 0], low) + dot(tables[left, 1], high)
    high, low = split(jnp.concatenate([mid[:length], mid[length:]], axis=1))
    out = dot(high, tables[right, 0]) + dot(low, tables[right, 0]) + dot(high, tables[right, 1])
    return out


def flux_of(real, imag):
    weight = 1.0 / (1.0 + (real * real + imag * imag) / (EDGE_SCALE * EDGE_SCALE))
    return real * weight, imag * weight


def kernel(n, obj_in, probe_in, amp_in, off_ref, cnt_ref, tab_in, out_ref, pout_ref,
           obj_ref, probe_ref, amp_ref, tab_ref, load_sem, cut, ext, pf, far, pw, pw_in, gext, patch, spill, ysend, yin, mar, ps, rbuf, po, ssem, rsem):
    tile, columns = obj_ref.shape[1:]
    length = pf.shape[-1]
    slots, modes = pf.shape[0], probe_ref.shape[0]
    block = 2 * tile
    bits = n.bit_length() - 1
    strips = length // LANES
    d, o = lax.axis_index("diff"), lax.axis_index("obj")
    q = 1 - o
    has_low, has_high = d > 0, d < n - 1
    rank = 2 * d + o
    has_prev, has_next = rank > 0, rank < 2 * n - 1
    partner = {"diff": d, "obj": q}
    lower = {"diff": d - 1, "obj": o}
    upper = {"diff": d + 1, "obj": o}
    prev_tile = {"diff": d - 1 + o, "obj": q}
    next_tile = {"diff": d + o, "obj": q}
    bit = [lax.rem(d // (1 << k), 2) for k in range(bits)]
    cube = [{"diff": d + (1 - 2 * bit[k]) * (1 << k), "obj": o} for k in range(bits)]

    def remote(src, dst, index, device):
        return pltpu.make_async_remote_copy(
            src_ref=src, dst_ref=dst, send_sem=ssem.at[index], recv_sem=rsem.at[index],
            device_id=device, device_id_type=MESH)

    def rows(start, size):
        return pl.ds(pl.multiple_of(start, 8), size)

    def pick(shape, long, offset):
        far_at = lax.broadcasted_iota(jnp.int32, shape, long)
        near_at = lax.broadcasted_iota(jnp.int32, shape, 1 - long)
        return jnp.where(far_at - near_at == offset, 1.0, 0.0).astype(BF16)

    loads = [pltpu.make_async_copy(src, dst, load_sem.at[i]) for i, (src, dst) in enumerate(
        ((obj_in, obj_ref), (tab_in, tab_ref), (probe_in, probe_ref), (amp_in, amp_ref)))]
    for load in loads:
        load.start()

    barrier = pltpu.get_barrier_semaphore()

    def greet(device):
        pl.semaphore_signal(barrier, inc=1, device_id=device, device_id_type=MESH)

    greet(partner)
    for k in range(bits):
        greet(cube[k])
    other = d - 1 + 2 * bit[0]
    cross = d - 1 + 2 * o
    has_other = (other >= 0) & (other < n)
    has_cross = (cross >= 0) & (cross < n)

    @pl.when(has_other)
    def _():
        greet({"diff": other, "obj": o})

    @pl.when(has_cross)
    def _():
        greet({"diff": cross, "obj": q})

    pl.semaphore_wait(barrier, 1 + bits + has_other.astype(jnp.int32) + has_cross.astype(jnp.int32))

    to_partner, direct, relay = [], [], []
    for c in range(2):
        to_partner.append(remote(obj_in.at[c], ext.at[c, rows(o * tile, tile)], c, partner))
        direct.append(remote(obj_in.at[c], ext.at[c, rows(block + o * tile, tile)], 2 + c, lower))
        relay.append(remote(ext.at[c, rows(q * tile, tile)], ext.at[c, rows(block + q * tile, tile)], 4 + c, lower))
        to_partner[c].start()
    for c in range(2):
        pl.when(has_low)(direct[c].start)
    for load in loads:
        load.wait()
    for c in range(2):
        ext[c, rows(o * tile, tile), :] = obj_ref[c]

    @pl.when(d == n - 1)
    def _():
        for c in range(2):
            ext[c, block:, :] = jnp.zeros((block, columns), F32)

    @pl.when(d == 0)
    def _():
        spill[...] = jnp.zeros_like(spill)

    @pl.when(rank == 0)
    def _():
        mar[:, :EDGE, :] = jnp.zeros((2, EDGE, columns), F32)

    @pl.when(rank == 2 * n - 1)
    def _():
        mar[:, EDGE + tile:, :] = jnp.zeros((2, EDGE, columns), F32)

    for c in range(2):
        to_partner[c].wait_recv()
        pl.when(has_low)(relay[c].start)
    def cut_columns(half):
        for s in range(slots):
            column_pick = pick((columns, length), 0, off_ref[s, 1])
            for c in range(2):
                high, low = split(ext[c, half * block:(half + 1) * block, :])
                cut[s, c, half * block:(half + 1) * block, :] = dot(high, column_pick) + dot(low, column_pick)

    cut_columns(0)
    for c in range(2):
        pl.when(has_high)(direct[c].wait_recv)
    for c in range(2):
        pl.when(has_high)(relay[c].wait_recv)
    cut_columns(1)

    base = 6 + slots
    total = ps.shape[0] // modes
    sums, shares, keeps, places = [], [], [], []
    index = base + 5
    for g in range(modes):
        rest = list(range(1, bits))
        turn = g % max(1, len(rest))
        order = [0] + rest[turn:] + rest[:turn]
        start, size, filled = g * total, total, g * total
        sums.append([])
        shares.append([])
        keeps.append([])
        places.append([])
        for k in order:
            half = size // 2
            sums[g].append(remote(ps.at[rows(start + (1 - bit[k]) * half, half)],
                                  rbuf.at[pl.ds(filled, half)], index, cube[k]))
            places[g].append((filled, half))
            start, size = start + bit[k] * half, half
            keeps[g].append(rows(start, size))
            filled += half
            index += 1
        for step, k in enumerate(order):
            mine = po.at[keeps[g][step]]
            shares[g].append(remote(mine, mine, index, cube[k]))
            index += 1

    power_copy = []
    for s in range(slots):
        row_pick = pick((length, 2 * block), 1, off_ref[s, 0])
        for c in range(2):
            high, low = split(cut[s, c])
            pf[s, c] = dot(row_pick, high) + dot(row_pick, low)
        pw[s] = jnp.zeros((length, length), F32)

        @pl.loop(0, modes)
        def _(m, s=s):
            pr, pi = probe_ref[m, 0], probe_ref[m, 1]
            fr, fi = pf[s, 0], pf[s, 1]
            wave = transform(pr * fr - pi * fi, pr * fi + pi * fr, tab_ref, 0, 1, length)
            far[s, m] = wave
            real, imag = wave[:, :length], wave[:, length:]
            pw[s] += real * real + imag * imag

        power_copy.append(remote(pw.at[s], pw_in.at[s], 6 + s, partner))
        power_copy[s].start()

    for s in range(slots):
        used = jnp.full((1, length), cnt_ref[d], jnp.int32)
        weight = jnp.where(used > s, 1.0, 0.0).astype(F32)
        power_copy[s].wait_recv()
        patch[...] = jnp.zeros_like(patch)
        pw_in[s] = amp_ref[s] / jnp.sqrt(pw[s] + pw_in[s] + 1.0) - 1.0

        @pl.loop(0, modes)
        def _(m, s=s, weight=weight):
            pr, pi = probe_ref[m, 0], probe_ref[m, 1]
            fr, fi = pf[s, 0], pf[s, 1]
            factor = pw_in[s]
            back = transform(far[s, m, :, :length] * factor, far[s, m, :, length:] * factor,
                             tab_ref, 1, 0, length)
            real, imag = back[:, :length] * weight, back[:, length:] * weight
            patch[0] += pr * real + pi * imag
            patch[1] += pr * imag - pi * real
            grad_r = fr * real + fi * imag
            grad_i = fr * imag - fi * real
            for c, grad in ((0, grad_r), (1, grad_i)):
                for h in range(strips):
                    at = rows(((m * 2 + c) * strips + h) * length, length)
                    if s == 0:
                        ps[at, :] = grad[:, h * LANES:(h + 1) * LANES]
                    else:
                        ps[at, :] += grad[:, h * LANES:(h + 1) * LANES]

            if s == slots - 1:
                for g in range(modes):
                    pl.when(m == g)(sums[g][0].start)

        row_place = pick((2 * block, length), 0, off_ref[s, 0])
        column_place = pick((length, columns), 1, off_ref[s, 1])
        for c in range(2):
            high, low = split(patch[c])
            high, low = split(dot(row_place, high) + dot(row_place, low))
            placed = dot(high, column_place) + dot(low, column_place)
            if s == 0:
                gext[c] = placed
            else:
                gext[c] += placed

    spill_copy = [remote(gext.at[:, rows(block + t * tile, tile)], spill.at[h], base + h, upper)
                  for h, t in ((0, q), (1, o))]
    for copy in spill_copy:
        pl.when(has_high)(copy.start)

    def add_sum(g, k):
        sums[g][k].wait_recv()
        at, size = places[g][k]
        ps[keeps[g][k], :] += rbuf[at:at + size, :]

    pl.when(has_low)(spill_copy[0].wait_recv)
    ysend[...] = gext[:, rows(q * tile, tile), :] + spill[0]
    to_owner = remote(ysend, yin, base + 2, partner)
    to_owner.start()
    for k in range(bits):
        for g in range(modes):
            add_sum(g, k)
            if k + 1 < bits:
                sums[g][k + 1].start()
            else:
                po[keeps[g][k], :] = ps[keeps[g][k], :]
                shares[g][k].start()

    pl.when(has_low)(spill_copy[1].wait_recv)
    to_owner.wait_recv()
    mar[:, EDGE:EDGE + tile, :] = obj_ref[...] + OBJECT_STEP * (gext[:, rows(o * tile, tile), :] + spill[1] + yin[...])
    up = remote(mar.at[:, pl.ds(EDGE, EDGE)], mar.at[:, pl.ds(EDGE + tile, EDGE)], base + 3, prev_tile)
    down = remote(mar.at[:, pl.ds(tile, EDGE)], mar.at[:, pl.ds(0, EDGE)], base + 4, next_tile)
    pl.when(has_prev)(up.start)
    pl.when(has_next)(down.start)
    left = list(range(bits - 1, -1, -1))

    def share():
        if left:
            k = left.pop(0)
            for g in range(modes):
                shares[g][k].wait_recv()
                if left:
                    shares[g][left[0]].start()

    share()
    pl.when(has_next)(up.wait_recv)
    pl.when(has_prev)(down.wait_recv)

    tall = tile + 2 * EDGE
    ids = rank * tile - EDGE + lax.broadcasted_iota(jnp.int32, (tall, columns), 0)
    below = (ids >= 0) & (ids + 1 < 2 * n * tile)
    beside = lax.broadcasted_iota(jnp.int32, (tall, columns), 1) < columns - 1
    u_r, u_i = mar[0], mar[1]
    for sweep in range(PASSES):
        v_r, v_i = flux_of(pltpu.roll(u_r, tall - 1, 0) - u_r, pltpu.roll(u_i, tall - 1, 0) - u_i)
        h_r, h_i = flux_of(pltpu.roll(u_r, columns - 1, 1) - u_r, pltpu.roll(u_i, columns - 1, 1) - u_i)

        def moved(v, h):
            v = jnp.where(below, v, 0.0)
            h = jnp.where(beside, h, 0.0)
            return DIFFUSION_RATE * ((v - pltpu.roll(v, 1, 0)) + (h - pltpu.roll(h, 1, 1)))

        u_r, u_i = u_r + moved(v_r, h_r), u_i + moved(v_i, h_i)
        share()
    out_ref[0] = u_r[EDGE:EDGE + tile]
    out_ref[1] = u_i[EDGE:EDGE + tile]
    while left:
        share()
    for m in range(modes):
        for c in range(2):
            for h in range(strips):
                at = ((m * 2 + c) * strips + h) * length
                lanes = slice(h * LANES, (h + 1) * LANES)
                pout_ref[m, c, :, lanes] = probe_ref[m, c, :, lanes] + po[at:at + length, :] / n

    for copy in to_partner + power_copy + sum(sums, []) + sum(shares, []) + [to_owner]:
        copy.wait_send()
    for copy in direct + relay:
        pl.when(has_low)(copy.wait_send)
    for copy in spill_copy:
        pl.when(has_high)(copy.wait_send)
    pl.when(has_prev)(up.wait_send)
    pl.when(has_next)(down.wait_send)


def body(n, object_field, probe_modes, amplitudes, offsets, counts):
    _, tile, columns = object_field.shape
    modes, _, length, _ = probe_modes.shape
    slots = amplitudes.shape[0]
    bits = n.bit_length() - 1
    block = 2 * tile
    copies = 11 + slots + 2 * bits * modes
    vmem = pl.BlockSpec(memory_space=pltpu.VMEM)
    hbm = pl.BlockSpec(memory_space=pltpu.HBM)
    smem = pl.BlockSpec(memory_space=pltpu.SMEM)
    tables = jnp.asarray(dft_blocks(length))
    return pl.pallas_call(
        functools.partial(kernel, n),
        out_shape=(
            jax.ShapeDtypeStruct(object_field.shape, F32),
            jax.ShapeDtypeStruct(probe_modes.shape, F32),
        ),
        in_specs=[hbm, hbm, hbm, smem, smem, hbm],
        out_specs=(vmem, vmem),
        scratch_shapes=[
            pltpu.VMEM(object_field.shape, F32),
            pltpu.VMEM(probe_modes.shape, F32),
            pltpu.VMEM(amplitudes.shape, F32),
            pltpu.VMEM(tables.shape, BF16),
            pltpu.SemaphoreType.DMA((4,)),
            pltpu.VMEM((slots, 2, 2 * block, length), F32),
            pltpu.VMEM((2, 2 * block, columns), F32),
            pltpu.VMEM((slots, 2, length, length), F32),
            pltpu.VMEM((slots, modes, length, 2 * length), F32),
            pltpu.VMEM((slots, length, length), F32),
            pltpu.VMEM((slots, length, length), F32),
            pltpu.VMEM((2, 2 * block, columns), F32),
            pltpu.VMEM((2, length, length), F32),
            pltpu.VMEM((2, 2, tile, columns), F32),
            pltpu.VMEM((2, tile, columns), F32),
            pltpu.VMEM((2, tile, columns), F32),
            pltpu.VMEM((2, tile + 2 * EDGE, columns), F32),
            pltpu.VMEM((modes * 2 * length * length // LANES, LANES), F32),
            pltpu.VMEM((modes * 2 * length * length // LANES, LANES), F32),
            pltpu.VMEM((modes * 2 * length * length // LANES, LANES), F32),
            pltpu.SemaphoreType.DMA((copies,)),
            pltpu.SemaphoreType.DMA((copies,)),
        ],
        compiler_params=pltpu.CompilerParams(
            collective_id=0, has_side_effects=True, vmem_limit_bytes=48 * 2**20
        ),
    )(object_field, probe_modes, amplitudes, offsets, counts, tables)


def solution(mesh):
    placed = (
        P(None, ("diff", "obj"), None),
        P("obj", None, None, None),
        P("diff", None, None),
        P("diff", None),
        P(),
    )
    return jax.shard_map(
        functools.partial(body, mesh.shape["diff"]),
        mesh=mesh,
        in_specs=placed,
        out_specs=(P(None, ("diff", "obj"), None), P("obj", None, None, None)),
        check_vma=False,
    )
```

```python
import functools

import jax
import jax.numpy as jnp
import ml_dtypes
import numpy as np
from jax import lax
from jax.experimental import pallas as pl
from jax.experimental.pallas import tpu as pltpu
from jax.sharding import PartitionSpec as P

PASSES = 3
EDGE_SCALE = 1.0
DIFFUSION_RATE = 0.2
OBJECT_STEP = 0.25
EDGE = 8
LANES = 128
MESH = pl.DeviceIdType.MESH
BF16 = jnp.bfloat16
F32 = jnp.float32


def dft_blocks(length):
    ladder = np.arange(length)
    angle = (ladder[:, None] * ladder[None, :] % length) * (2.0 * np.pi / length)
    cosine = np.cos(angle) / np.sqrt(length)
    sine = np.sin(angle) / np.sqrt(length)
    forward = np.block([[cosine, sine], [-sine, cosine]]).astype(np.float32)

    def halves(table):
        high = table.astype(ml_dtypes.bfloat16)
        low = (table - high.astype(np.float32)).astype(ml_dtypes.bfloat16)
        return np.stack([high, low])

    return np.stack([halves(forward), halves(forward.T)])


def split(value):
    high = value.astype(BF16)
    return high, (value - high.astype(F32)).astype(BF16)


def dot(a, b):
    return jnp.dot(a, b, preferred_element_type=F32)


def transform(real, imag, tables, left, right, length):
    high, low = split(jnp.concatenate([real, imag], axis=0))
    mid = dot(tables[left, 0], high) + dot(tables[left, 0], low) + dot(tables[left, 1], high)
    high, low = split(jnp.concatenate([mid[:length], mid[length:]], axis=1))
    out = dot(high, tables[right, 0]) + dot(low, tables[right, 0]) + dot(high, tables[right, 1])
    return out


def flux_of(real, imag):
    weight = 1.0 / (1.0 + (real * real + imag * imag) / (EDGE_SCALE * EDGE_SCALE))
    return real * weight, imag * weight


def kernel(n, obj_in, probe_in, amp_in, off_ref, cnt_ref, tab_in, out_ref, pout_ref,
           obj_ref, probe_ref, amp_ref, tab_ref, load_sem, cut, ext, pf, far, pw, pw_in, gext, patch, spill, ysend, yin, mar, ps, rbuf, po, ssem, rsem):
    tile, columns = obj_ref.shape[1:]
    length = pf.shape[-1]
    slots, modes = pf.shape[0], probe_ref.shape[0]
    block = 2 * tile
    bits = n.bit_length() - 1
    strips = length // LANES
    d, o = lax.axis_index("diff"), lax.axis_index("obj")
    q = 1 - o
    has_low, has_high = d > 0, d < n - 1
    rank = 2 * d + o
    has_prev, has_next = rank > 0, rank < 2 * n - 1
    partner = {"diff": d, "obj": q}
    lower = {"diff": d - 1, "obj": o}
    upper = {"diff": d + 1, "obj": o}
    prev_tile = {"diff": d - 1 + o, "obj": q}
    next_tile = {"diff": d + o, "obj": q}
    bit = [lax.rem(d // (1 << k), 2) for k in range(bits)]
    cube = [{"diff": d + (1 - 2 * bit[k]) * (1 << k), "obj": o} for k in range(bits)]

    def remote(src, dst, index, device):
        return pltpu.make_async_remote_copy(
            src_ref=src, dst_ref=dst, send_sem=ssem.at[index], recv_sem=rsem.at[index],
            device_id=device, device_id_type=MESH)

    def rows(start, size):
        return pl.ds(pl.multiple_of(start, 8), size)

    def pick(shape, long, offset):
        far_at = lax.broadcasted_iota(jnp.int32, shape, long)
        near_at = lax.broadcasted_iota(jnp.int32, shape, 1 - long)
        return jnp.where(far_at - near_at == offset, 1.0, 0.0).astype(BF16)

    loads = [pltpu.make_async_copy(src, dst, load_sem.at[i]) for i, (src, dst) in enumerate(
        ((obj_in, obj_ref), (tab_in, tab_ref), (probe_in, probe_ref), (amp_in, amp_ref)))]
    for load in loads:
        load.start()

    barrier = pltpu.get_barrier_semaphore()

    def greet(device):
        pl.semaphore_signal(barrier, inc=1, device_id=device, device_id_type=MESH)

    greet(partner)
    for k in range(bits):
        greet(cube[k])
    other = d - 1 + 2 * bit[0]
    cross = d - 1 + 2 * o
    has_other = (other >= 0) & (other < n)
    has_cross = (cross >= 0) & (cross < n)

    @pl.when(has_other)
    def _():
        greet({"diff": other, "obj": o})

    @pl.when(has_cross)
    def _():
        greet({"diff": cross, "obj": q})

    pl.semaphore_wait(barrier, 1 + bits + has_other.astype(jnp.int32) + has_cross.astype(jnp.int32))

    to_partner, direct, relay = [], [], []
    for c in range(2):
        to_partner.append(remote(obj_in.at[c], ext.at[c, rows(o * tile, tile)], c, partner))
        direct.append(remote(obj_in.at[c], ext.at[c, rows(block + o * tile, tile)], 2 + c, lower))
        relay.append(remote(ext.at[c, rows(q * tile, tile)], ext.at[c, rows(block + q * tile, tile)], 4 + c, lower))
        to_partner[c].start()
    for c in range(2):
        pl.when(has_low)(direct[c].start)
    for load in loads:
        load.wait()
    for c in range(2):
        ext[c, rows(o * tile, tile), :] = obj_ref[c]

    @pl.when(d == n - 1)
    def _():
        for c in range(2):
            ext[c, block:, :] = jnp.zeros((block, columns), F32)

    @pl.when(d == 0)
    def _():
        spill[...] = jnp.zeros_like(spill)

    @pl.when(rank == 0)
    def _():
        mar[:, :EDGE, :] = jnp.zeros((2, EDGE, columns), F32)

    @pl.when(rank == 2 * n - 1)
    def _():
        mar[:, EDGE + tile:, :] = jnp.zeros((2, EDGE, columns), F32)

    for c in range(2):
        to_partner[c].wait_recv()
        pl.when(has_low)(relay[c].start)
    def cut_columns(half):
        for s in range(slots):
            column_pick = pick((columns, length), 0, off_ref[s, 1])
            for c in range(2):
                high, low = split(ext[c, half * block:(half + 1) * block, :])
                cut[s, c, half * block:(half + 1) * block, :] = dot(high, column_pick) + dot(low, column_pick)

    cut_columns(0)
    for c in range(2):
        pl.when(has_high)(direct[c].wait_recv)
    for c in range(2):
        pl.when(has_high)(relay[c].wait_recv)
    cut_columns(1)

    base = 6 + slots
    total = ps.shape[0] // modes
    sums, shares, keeps, places = [], [], [], []
    index = base + 5
    for g in range(modes):
        rest = list(range(1, bits))
        turn = g % max(1, len(rest))
        order = [0] + rest[turn:] + rest[:turn]
        start, size, filled = g * total, total, g * total
        sums.append([])
        shares.append([])
        keeps.append([])
        places.append([])
        for k in order:
            half = size // 2
            sums[g].append(remote(ps.at[rows(start + (1 - bit[k]) * half, half)],
                                  rbuf.at[pl.ds(filled, half)], index, cube[k]))
            places[g].append((filled, half))
            start, size = start + bit[k] * half, half
            keeps[g].append(rows(start, size))
            filled += half
            index += 1
        for step, k in enumerate(order):
            mine = po.at[keeps[g][step]]
            shares[g].append(remote(mine, mine, index, cube[k]))
            index += 1

    power_copy = []
    for s in range(slots):
        row_pick = pick((length, 2 * block), 1, off_ref[s, 0])
        for c in range(2):
            high, low = split(cut[s, c])
            pf[s, c] = dot(row_pick, high) + dot(row_pick, low)
        pw[s] = jnp.zeros((length, length), F32)

        @pl.loop(0, modes)
        def _(m, s=s):
            pr, pi = probe_ref[m, 0], probe_ref[m, 1]
            fr, fi = pf[s, 0], pf[s, 1]
            wave = transform(pr * fr - pi * fi, pr * fi + pi * fr, tab_ref, 0, 1, length)
            far[s, m] = wave
            real, imag = wave[:, :length], wave[:, length:]
            pw[s] += real * real + imag * imag

        power_copy.append(remote(pw.at[s], pw_in.at[s], 6 + s, partner))
        power_copy[s].start()

    for s in range(slots):
        used = jnp.full((1, length), cnt_ref[d], jnp.int32)
        weight = jnp.where(used > s, 1.0, 0.0).astype(F32)
        power_copy[s].wait_recv()
        patch[...] = jnp.zeros_like(patch)
        pw_in[s] = amp_ref[s] / jnp.sqrt(pw[s] + pw_in[s] + 1.0) - 1.0

        @pl.loop(0, modes)
        def _(m, s=s, weight=weight):
            pr, pi = probe_ref[m, 0], probe_ref[m, 1]
            fr, fi = pf[s, 0], pf[s, 1]
            factor = pw_in[s]
            back = transform(far[s, m, :, :length] * factor, far[s, m, :, length:] * factor,
                             tab_ref, 1, 0, length)
            real, imag = back[:, :length] * weight, back[:, length:] * weight
            patch[0] += pr * real + pi * imag
            patch[1] += pr * imag - pi * real
            grad_r = fr * real + fi * imag
            grad_i = fr * imag - fi * real
            for c, grad in ((0, grad_r), (1, grad_i)):
                for h in range(strips):
                    at = rows(((m * 2 + c) * strips + h) * length, length)
                    if s == 0:
                        ps[at, :] = grad[:, h * LANES:(h + 1) * LANES]
                    else:
                        ps[at, :] += grad[:, h * LANES:(h + 1) * LANES]

            if s == slots - 1:
                for g in range(modes):
                    pl.when(m == g)(sums[g][0].start)

        row_place = pick((2 * block, length), 0, off_ref[s, 0])
        column_place = pick((length, columns), 1, off_ref[s, 1])
        for c in range(2):
            high, low = split(patch[c])
            high, low = split(dot(row_place, high) + dot(row_place, low))
            placed = dot(high, column_place) + dot(low, column_place)
            if s == 0:
                gext[c] = placed
            else:
                gext[c] += placed

    spill_copy = [remote(gext.at[:, rows(block + t * tile, tile)], spill.at[h], base + h, upper)
                  for h, t in ((0, q), (1, o))]
    pl.when(has_high)(spill_copy[0].start)

    def add_sum(g, k):
        sums[g][k].wait_recv()
        at, size = places[g][k]
        ps[keeps[g][k], :] += rbuf[at:at + size, :]

    to_owner = remote(ysend, yin, base + 2, partner)
    for k in range(bits):
        for g in range(modes):
            add_sum(g, k)
            if k + 1 < bits:
                sums[g][k + 1].start()
            else:
                po[keeps[g][k], :] = ps[keeps[g][k], :]
                shares[g][k].start()
        if k == 0:
            pl.when(has_high)(spill_copy[1].start)
            pl.when(has_low)(spill_copy[0].wait_recv)
            ysend[...] = gext[:, rows(q * tile, tile), :] + spill[0]
            to_owner.start()

    pl.when(has_low)(spill_copy[1].wait_recv)
    to_owner.wait_recv()
    mar[:, EDGE:EDGE + tile, :] = obj_ref[...] + OBJECT_STEP * (gext[:, rows(o * tile, tile), :] + spill[1] + yin[...])
    up = remote(mar.at[:, pl.ds(EDGE, EDGE)], mar.at[:, pl.ds(EDGE + tile, EDGE)], base + 3, prev_tile)
    down = remote(mar.at[:, pl.ds(tile, EDGE)], mar.at[:, pl.ds(0, EDGE)], base + 4, next_tile)
    pl.when(has_prev)(up.start)
    pl.when(has_next)(down.start)
    left = list(range(bits - 1, -1, -1))

    def share():
        if left:
            k = left.pop(0)
            for g in range(modes):
                shares[g][k].wait_recv()
                if left:
                    shares[g][left[0]].start()

    share()
    pl.when(has_next)(up.wait_recv)
    pl.when(has_prev)(down.wait_recv)

    tall = tile + 2 * EDGE
    ids = rank * tile - EDGE + lax.broadcasted_iota(jnp.int32, (tall, columns), 0)
    below = (ids >= 0) & (ids + 1 < 2 * n * tile)
    beside = lax.broadcasted_iota(jnp.int32, (tall, columns), 1) < columns - 1
    u_r, u_i = mar[0], mar[1]
    for sweep in range(PASSES):
        v_r, v_i = flux_of(pltpu.roll(u_r, tall - 1, 0) - u_r, pltpu.roll(u_i, tall - 1, 0) - u_i)
        h_r, h_i = flux_of(pltpu.roll(u_r, columns - 1, 1) - u_r, pltpu.roll(u_i, columns - 1, 1) - u_i)

        def moved(v, h):
            v = jnp.where(below, v, 0.0)
            h = jnp.where(beside, h, 0.0)
            return DIFFUSION_RATE * ((v - pltpu.roll(v, 1, 0)) + (h - pltpu.roll(h, 1, 1)))

        u_r, u_i = u_r + moved(v_r, h_r), u_i + moved(v_i, h_i)
        share()
    out_ref[0] = u_r[EDGE:EDGE + tile]
    out_ref[1] = u_i[EDGE:EDGE + tile]
    while left:
        share()
    for m in range(modes):
        for c in range(2):
            for h in range(strips):
                at = ((m * 2 + c) * strips + h) * length
                lanes = slice(h * LANES, (h + 1) * LANES)
                pout_ref[m, c, :, lanes] = probe_ref[m, c, :, lanes] + po[at:at + length, :] / n

    for copy in to_partner + power_copy + sum(sums, []) + sum(shares, []) + [to_owner]:
        copy.wait_send()
    for copy in direct + relay:
        pl.when(has_low)(copy.wait_send)
    for copy in spill_copy:
        pl.when(has_high)(copy.wait_send)
    pl.when(has_prev)(up.wait_send)
    pl.when(has_next)(down.wait_send)


def body(n, object_field, probe_modes, amplitudes, offsets, counts):
    _, tile, columns = object_field.shape
    modes, _, length, _ = probe_modes.shape
    slots = amplitudes.shape[0]
    bits = n.bit_length() - 1
    block = 2 * tile
    copies = 11 + slots + 2 * bits * modes
    vmem = pl.BlockSpec(memory_space=pltpu.VMEM)
    hbm = pl.BlockSpec(memory_space=pltpu.HBM)
    smem = pl.BlockSpec(memory_space=pltpu.SMEM)
    tables = jnp.asarray(dft_blocks(length))
    return pl.pallas_call(
        functools.partial(kernel, n),
        out_shape=(
            jax.ShapeDtypeStruct(object_field.shape, F32),
            jax.ShapeDtypeStruct(probe_modes.shape, F32),
        ),
        in_specs=[hbm, hbm, hbm, smem, smem, hbm],
        out_specs=(vmem, vmem),
        scratch_shapes=[
            pltpu.VMEM(object_field.shape, F32),
            pltpu.VMEM(probe_modes.shape, F32),
            pltpu.VMEM(amplitudes.shape, F32),
            pltpu.VMEM(tables.shape, BF16),
            pltpu.SemaphoreType.DMA((4,)),
            pltpu.VMEM((slots, 2, 2 * block, length), F32),
            pltpu.VMEM((2, 2 * block, columns), F32),
            pltpu.VMEM((slots, 2, length, length), F32),
            pltpu.VMEM((slots, modes, length, 2 * length), F32),
            pltpu.VMEM((slots, length, length), F32),
            pltpu.VMEM((slots, length, length), F32),
            pltpu.VMEM((2, 2 * block, columns), F32),
            pltpu.VMEM((2, length, length), F32),
            pltpu.VMEM((2, 2, tile, columns), F32),
            pltpu.VMEM((2, tile, columns), F32),
            pltpu.VMEM((2, tile, columns), F32),
            pltpu.VMEM((2, tile + 2 * EDGE, columns), F32),
            pltpu.VMEM((modes * 2 * length * length // LANES, LANES), F32),
            pltpu.VMEM((modes * 2 * length * length // LANES, LANES), F32),
            pltpu.VMEM((modes * 2 * length * length // LANES, LANES), F32),
            pltpu.SemaphoreType.DMA((copies,)),
            pltpu.SemaphoreType.DMA((copies,)),
        ],
        compiler_params=pltpu.CompilerParams(
            collective_id=0, has_side_effects=True, vmem_limit_bytes=48 * 2**20
        ),
    )(object_field, probe_modes, amplitudes, offsets, counts, tables)


def solution(mesh):
    placed = (
        P(None, ("diff", "obj"), None),
        P("obj", None, None, None),
        P("diff", None, None),
        P("diff", None),
        P(),
    )
    return jax.shard_map(
        functools.partial(body, mesh.shape["diff"]),
        mesh=mesh,
        in_specs=placed,
        out_specs=(P(None, ("diff", "obj"), None), P("obj", None, None, None)),
        check_vma=False,
    )
```
